32 devices in a mesh: feat: 2 (over core), tok: 16 (over z, y, x).
Axes of the slice: x: 2, y: 2, z: 4, core: 2. Of those that a mesh axis runs over, the one named last changes fastest.
Arguments:
- activations: bfloat16 [4096, 28672], P('tok', 'feat'), may hold values from -160 to 160
- dense_rows: float32 [64, 28672], P(None, 'feat'), may hold values from -6 to 6
- targets: float32 [4096, 64], P('tok'), may hold values from -6 to 6
Outputs:
- pruned_rows: float32 [64, 28672], P(None, 'feat')
The draws below stay inside these ranges and needn't reach their ends.
All inputs are finite; a program needn't handle non-finite values.
Results may differ from the reference program's by a relative error of at most 0.0055.
Values may be sent and summed in bfloat16 or wider, within the bound.
No kernel may reach another device: no remote copies, remote signals or barrier semaphores. Data moves between devices by JAX's collectives and lax.ppermute only.
A program may use at most 64 MiB of HBM per device.

```python
import math
import jax
import jax.numpy as jnp
from jax import lax

DIN = 28672
ROWS = 64
ITERS = 4
TOKENS = 4096


def draw_activations(key, part):
    key_cols = jax.random.fold_in(key, 11)
    key_vals = jax.random.fold_in(key, 12)
    position = jnp.arange(DIN, dtype=jnp.float32) / DIN
    spread = jnp.exp(jax.random.uniform(key_cols, (DIN,), jnp.float32, math.log(0.3), math.log(3.0)))
    values = jax.random.truncated_normal(key_vals, -4.0, 4.0, (TOKENS, DIN), jnp.float32)
    column_scale = spread * jnp.power(3.0, position)
    return (values * column_scale[None, :]).astype(jnp.bfloat16)


def block_levels(rng, dims, shards, smallest, high):
    def one(dim, parts):
        heights = jax.random.uniform(jax.random.fold_in(jax.random.fold_in(rng, 6), dim), (parts,), jnp.float32, smallest / len(shards), high / len(shards))
        return jnp.repeat(jnp.exp(heights), dims[dim] // parts).reshape((-1,) + (1,) * (len(dims) - dim - 1))

    loudness = one(*shards[0])
    for cut in shards[1:]:
        loudness = loudness * one(*cut)
    return loudness


def normal_values(stream_key, dims, deviation, limit, split=(), held_as=jnp.bfloat16):
    drawn = deviation * jax.random.normal(stream_key, dims, jnp.float32)
    if split:
        drawn = drawn * block_levels(stream_key, dims, split, -0.22, 0.18)
    return jnp.clip(drawn, -limit, limit).astype(held_as)


def setup_inputs(seed: int = 0) -> dict:
    key_of = jax.random.split(jax.random.key(seed), 4)
    return {
        "activations": draw_activations(jax.random.fold_in(key_of[3], 71), 0),
        "dense_rows": normal_values(key_of[1], (ROWS, DIN), 1.0, 6.0, ((1, 2),), jnp.float32),
        "targets": normal_values(key_of[2], (TOKENS, ROWS), 1.0, 6.0, ((0, 16),), jnp.float32),
    }


step_size = 0.25
threshold = 0.2
epsilon = 1e-06

def momentum_terms(iterations):
    values = []
    current = 1.0
    for _ in range(iterations):
        upcoming = (1.0 + math.sqrt(1.0 + 4.0 * current * current)) / 2.0
        values.append((current - 1.0) / upcoming)
        current = upcoming
    return values

def reference(activations, dense_rows, targets):
    factor = DIN ** (-0.5)
    momentum = momentum_terms(ITERS)
    weights = dense_rows
    advance = dense_rows
    for iteration in range(ITERS):
        rounded = advance.astype(jnp.bfloat16)
        summed = lax.dot_general(activations, rounded, (((1,), (1,)), ((), ())), preferred_element_type=jnp.float32)
        residual = (factor * summed - targets).astype(jnp.bfloat16)
        gradient = lax.dot_general(residual, activations, (((0,), (0,)), ((), ())), preferred_element_type=jnp.float32)
        mean_square = jnp.sum(gradient * gradient) / (ROWS * DIN)
        moved = advance - step_size * gradient * lax.rsqrt(mean_square + epsilon)
        shrunk = jnp.sign(moved) * jnp.maximum(jnp.abs(moved) - threshold, 0.0)
        advance = shrunk + momentum[iteration] * (shrunk - weights)
        weights = shrunk
    return weights
```

```python
import math

import jax
import jax.numpy as jnp
from jax import lax
from jax.sharding import PartitionSpec as P

ITERS = 4
STEP = 0.25
THRESHOLD = 0.2
EPSILON = 1e-06
GROUP = 8
PARTS = 3


def momentum_terms(iterations):
    values = []
    current = 1.0
    for _ in range(iterations):
        upcoming = (1.0 + math.sqrt(1.0 + 4.0 * current * current)) / 2.0
        values.append((current - 1.0) / upcoming)
        current = upcoming
    return values


def swap(x, axis, bit):
    pairs = [(i, i ^ (1 << bit)) for i in range(lax.axis_size(axis))]
    return lax.ppermute(x, axis, pairs)


def bits_of(axis):
    return lax.axis_size(axis).bit_length() - 1


def flip_rows(x, dim, rows_bits):
    shape = x.shape
    index = lax.axis_index("tok")
    size = shape[dim]
    for bit in range(rows_bits):
        half = size >> (bit + 1)
        cut = shape[:dim] + (size // (2 * half), 2, half) + shape[dim + 1 :]
        y = x.reshape(cut)
        x = jnp.where((index >> bit) & 1 == 1, jnp.flip(y, dim + 1), y).reshape(shape)
    return x


def total(pieces, rows_bits):
    count = len(pieces)
    orders = [[(p + s) % rows_bits for s in range(rows_bits)] for p in range(count)]
    current = list(pieces)
    left = [list(range(rows_bits)) for _ in pieces]
    for stage in range(rows_bits):
        sent = []
        for p in range(count):
            dim = left[p].index(orders[p][stage])
            other = lax.index_in_dim(current[p], 1, dim, keepdims=False).astype(jnp.bfloat16)
            sent.append(swap(other, "tok", orders[p][stage]))
        for p in range(count):
            dim = left[p].index(orders[p][stage])
            kept = lax.index_in_dim(current[p], 0, dim, keepdims=False)
            current[p] = kept + sent[p].astype(jnp.float32)
            left[p].pop(dim)
    for bit in range(rows_bits, bits_of("tok")):
        low = [c.astype(jnp.bfloat16) for c in current]
        sent = [swap(c, "tok", bit) for c in low]
        current = [a.astype(jnp.float32) + b.astype(jnp.float32) for a, b in zip(low, sent)]
    current = [c.astype(jnp.bfloat16) for c in current]
    for stage in reversed(range(rows_bits)):
        sent = [swap(current[p], "tok", orders[p][stage]) for p in range(count)]
        for p in range(count):
            bit = orders[p][stage]
            dim = sum(1 for b in left[p] if b < bit)
            left[p].insert(dim, bit)
            current[p] = jnp.stack([current[p], sent[p]], dim)
    return current


def shards(activations, dense_rows, targets):
    rows = dense_rows.shape[0]
    features = dense_rows.shape[1] * lax.axis_size("feat")
    entries = rows * features
    factor = features ** (-0.5)
    momentum = momentum_terms(ITERS)
    rows_bits = min(bits_of("tok"), (rows // GROUP).bit_length() - 1)
    units = dense_rows.shape[1] // 256
    edges = [256 * (units * p // PARTS) for p in range(PARTS + 1)]
    spans = list(zip(edges[:-1], edges[1:]))
    wanted = flip_rows(targets, 1, rows_bits)
    start = flip_rows(dense_rows, 0, rows_bits)
    weights = [start[:, a:b] for a, b in spans]
    ahead = weights
    blocks = [activations[:, a:b] for a, b in spans]
    for iteration in range(ITERS):
        product = sum(
            lax.dot_general(
                block, part.astype(jnp.bfloat16), (((1,), (1,)), ((), ())), preferred_element_type=jnp.float32
            )
            for block, part in zip(blocks, ahead)
        )
        for bit in range(bits_of("feat")):
            product = product + swap(product, "feat", bit)
        residual = (factor * product - wanted).astype(jnp.bfloat16)
        pieces = [
            lax.dot_general(
                residual, block, (((0,), (0,)), ((), ())), preferred_element_type=jnp.float32
            ).reshape((2,) * rows_bits + (rows >> rows_bits, block.shape[1]))
            for block in blocks
        ]
        gradient = [
            g.reshape(rows, -1).astype(jnp.float32) for g in total(pieces, rows_bits)
        ]
        square = sum(jnp.sum(g * g) for g in gradient).reshape(1, 1)
        for bit in range(bits_of("feat")):
            square = square + swap(square, "feat", bit)
        scale = STEP * lax.rsqrt(square / entries + EPSILON)
        upcoming = []
        following = []
        for w, a, g in zip(weights, ahead, gradient):
            moved = a - scale * g
            shrunk = jnp.sign(moved) * jnp.maximum(jnp.abs(moved) - THRESHOLD, 0.0)
            following.append(shrunk + momentum[iteration] * (shrunk - w))
            upcoming.append(shrunk)
        weights, ahead = upcoming, following
    return flip_rows(jnp.concatenate(weights, 1), 0, rows_bits)


def solution(mesh):
    in_specs = (P("tok", "feat"), P(None, "feat"), P("tok", None))
    out_specs = P(None, "feat")
    return jax.shard_map(shards, mesh=mesh, in_specs=in_specs, out_specs=out_specs, check_vma=False)
```

```python
import functools
import math

import jax
import jax.numpy as jnp
from jax import lax
from jax.experimental import pallas as pl
from jax.experimental.pallas import tpu as pltpu
from jax.sharding import PartitionSpec as P

ITERS = 4
STEP = 0.25
THRESHOLD = 0.2
EPSILON = 1e-06
GROUP = 8
PARTS = 3
VMEM_BYTES = 4 * 1024 * 1024

f32 = jnp.float32
bf16 = jnp.bfloat16


def momentum_terms(iterations):
    values = []
    current = 1.0
    for _ in range(iterations):
        upcoming = (1.0 + math.sqrt(1.0 + 4.0 * current * current)) / 2.0
        values.append((current - 1.0) / upcoming)
        current = upcoming
    return values


def swap(x, axis, bit):
    pairs = [(i, i ^ (1 << bit)) for i in range(lax.axis_size(axis))]
    return lax.ppermute(x, axis, pairs)


def bits_of(axis):
    return lax.axis_size(axis).bit_length() - 1


class Plan:
    def __init__(self, rows, columns):
        self.rows = rows
        self.columns = columns
        self.rows_bits = min(bits_of("tok"), (rows // GROUP).bit_length() - 1)
        self.places = 1 << self.rows_bits
        self.height = rows >> self.rows_bits
        self.unit = next(u for u in (512, 256, 128) if columns % u == 0)
        units = columns // self.unit
        edges = [units * p // PARTS for p in range(PARTS + 1)]
        self.spans = list(zip(edges[:-1], edges[1:]))
        self.widths = [(b - a) * self.unit for a, b in self.spans]
        self.orders = [[(p + s) % self.rows_bits for s in range(self.rows_bits)] for p in range(PARTS)]

    def bit_value(self, level):
        return self.places >> (level + 1)

    def arrangement(self, p):
        result = [0]
        for level in reversed(self.orders[p]):
            result = result + [g + self.bit_value(level) for g in result]
        return result

    def mask(self):
        index = lax.axis_index("tok")
        return sum(((index >> level) & 1) * self.bit_value(level) for level in range(self.rows_bits))

    def rearranged(self, x, places):
        h = self.height
        return jnp.concatenate([x[h * g : h * (g + 1)] for g in places], 0)

    def to_part(self, p, x):
        return self.rearranged(x, self.arrangement(p))

    def from_part(self, p, x):
        order = self.arrangement(p)
        return self.rearranged(x, [order.index(g) for g in range(self.places)])


def dot_nt(a, b):
    return lax.dot_general(a, b, (((1,), (1,)), ((), ())), preferred_element_type=f32)


def vmem(count):
    return [pl.BlockSpec(memory_space=pltpu.VMEM)] * count


PARAMS = pltpu.CompilerParams(vmem_limit_bytes=VMEM_BYTES)


def first_kernel(plan, mask_ref, dense_ref, act_ref, start_ref, product_ref):
    mask = mask_ref[0]
    h = plan.height
    total = jnp.zeros(product_ref.shape, f32)

    def step(i, total):
        columns = pl.ds(pl.multiple_of(i * plan.unit, plan.unit), plan.unit)
        groups = []
        for g in range(plan.places):
            rows = pl.ds(pl.multiple_of((g ^ mask) * h, h), h)
            groups.append(dense_ref[rows, columns])
        block = jnp.concatenate(groups, 0)
        start_ref[:, columns] = block
        return total + dot_nt(block.astype(bf16), act_ref[:, columns])

    product_ref[...] = lax.fori_loop(0, plan.columns // plan.unit, step, total, unroll=2)


def gradient_kernel(plan, factor, own_ref, other_ref, wanted_ref, act_ref, *outs):
    product = own_ref[...] + other_ref[...]
    residual = factor * product - wanted_ref[...]
    half = plan.rows // 2
    for p, (first, last) in enumerate(plan.spans):
        arranged = plan.to_part(p, residual).astype(bf16)
        keep_ref, send_ref = outs[2 * p], outs[2 * p + 1]

        def step(i, carry):
            source = pl.ds(pl.multiple_of((first + i) * plan.unit, plan.unit), plan.unit)
            target = pl.ds(pl.multiple_of(i * plan.unit, plan.unit), plan.unit)
            block = jnp.dot(arranged, act_ref[:, source], preferred_element_type=f32)
            keep_ref[:, target] = block[:half]
            send_ref[:, target] = block[half:].astype(bf16)
            return carry

        lax.fori_loop(0, last - first, step, 0, unroll=2)


def square_kernel(plan, *refs):
    *halves, out_ref = refs
    total = jnp.zeros((8, 128), f32)
    for ref in halves:

        def step(i, total):
            columns = pl.ds(pl.multiple_of(i * plan.unit, plan.unit), plan.unit)
            block = ref[:, columns].astype(f32)
            block = block * block
            for r in range(0, block.shape[0], 8):
                for c in range(0, plan.unit, 128):
                    total = total + block[r : r + 8, c : c + 128]
            return total

        total = lax.fori_loop(0, ref.shape[1] // plan.unit, step, total, unroll=2)
    out_ref[...] = total


def update_kernel(plan, momentum, last, *refs):
    if last:
        mask_ref, *refs = refs
    own_ref, other_ref, *refs = refs
    halves, refs = refs[: 2 * PARTS], refs[2 * PARTS :]
    if last:
        weights_ref, ahead_ref, out_ref = refs
    else:
        weights_ref, ahead_ref, act_ref, new_weights_ref, new_ahead_ref, product_ref = refs
        total = jnp.zeros(product_ref.shape, f32)
    mean_square = jnp.sum(own_ref[...] + other_ref[...], keepdims=True) / plan.entries
    scale = STEP * lax.rsqrt(mean_square + EPSILON)
    h = plan.height
    for p, (begin, end) in enumerate(plan.spans):
        kept_ref, came_ref = halves[2 * p], halves[2 * p + 1]

        def step(i, carry):
            source = pl.ds(pl.multiple_of(i * plan.unit, plan.unit), plan.unit)
            target = pl.ds(pl.multiple_of((begin + i) * plan.unit, plan.unit), plan.unit)
            gradient = jnp.concatenate([kept_ref[:, source].astype(f32), came_ref[:, source].astype(f32)], 0)
            gradient = plan.from_part(p, gradient)
            moved = ahead_ref[:, target] - scale * gradient
            shrunk = moved - jnp.clip(moved, -THRESHOLD, THRESHOLD)
            if last:
                for g in range(plan.places):
                    rows = pl.ds(pl.multiple_of((g ^ mask_ref[0]) * h, h), h)
                    out_ref[rows, target] = shrunk[h * g : h * (g + 1)]
                return carry
            ahead = shrunk + momentum * (shrunk - weights_ref[:, target])
            new_weights_ref[:, target] = shrunk
            new_ahead_ref[:, target] = ahead
            return carry + dot_nt(ahead.astype(bf16), act_ref[:, target])

        carried = lax.fori_loop(0, end - begin, step, 0 if last else total, unroll=2)
        if not last:
            total = carried
    if not last:
        product_ref[...] = total


def all_sum(plan, pieces):
    count = len(pieces)
    current = [kept for kept, _ in pieces]
    sends = [sent for _, sent in pieces]
    for stage in range(plan.rows_bits):
        came = [swap(sends[p], "tok", plan.orders[p][stage]) for p in range(count)]
        current = [c + r.astype(f32) for c, r in zip(current, came)]
        if stage + 1 < plan.rows_bits:
            middle = current[0].shape[0] // 2
            sends = [c[middle:].astype(bf16) for c in current]
            current = [c[:middle] for c in current]
    for bit in range(plan.rows_bits, bits_of("tok")):
        low = [c.astype(bf16) for c in current]
        came = [swap(c, "tok", bit) for c in low]
        current = [a.astype(f32) + b.astype(f32) for a, b in zip(low, came)]
    current = [c.astype(bf16) for c in current]
    for stage in reversed(range(plan.rows_bits)):
        came = [swap(current[p], "tok", plan.orders[p][stage]) for p in range(count)]
        if stage:
            current = [jnp.concatenate([a, b], 0) for a, b in zip(current, came)]
    return [x for pair in zip(current, came) for x in pair]


def across_features(x):
    count = bits_of("feat")
    for bit in range(count - 1):
        x = x + swap(x, "feat", bit)
    return x, swap(x, "feat", count - 1)


def shards(activations, dense_rows, targets):
    rows, columns = dense_rows.shape
    tokens = activations.shape[0]
    plan = Plan(rows, columns)
    features = columns * lax.axis_size("feat")
    plan.entries = rows * features
    factor = features ** (-0.5)
    momentum = momentum_terms(ITERS)
    mask = plan.mask()
    wanted = targets.T
    for level in range(plan.rows_bits):
        half = rows >> (level + 1)
        cut = wanted.reshape(-1, 2, half, tokens)
        bit = (lax.axis_index("tok") >> level) & 1
        wanted = jnp.where(bit == 1, cut[:, ::-1], cut).reshape(rows, tokens)
    mask = mask.reshape(1).astype(jnp.int32)
    smem = [pl.BlockSpec(memory_space=pltpu.SMEM)]
    state = jax.ShapeDtypeStruct((rows, columns), f32)
    small = jax.ShapeDtypeStruct((rows, tokens), f32)
    tile = jax.ShapeDtypeStruct((8, 128), f32)
    halves = []
    for width in plan.widths:
        halves.append(jax.ShapeDtypeStruct((rows // 2, width), f32))
        halves.append(jax.ShapeDtypeStruct((rows // 2, width), bf16))

    ahead, product = pl.pallas_call(
        functools.partial(first_kernel, plan),
        out_shape=(state, small),
        in_specs=smem + vmem(2),
        out_specs=tuple(vmem(2)),
        compiler_params=PARAMS,
        name="first",
    )(mask, dense_rows, activations)
    weights = ahead
    for iteration in range(ITERS):
        own, other = across_features(product)
        pieces = pl.pallas_call(
            functools.partial(gradient_kernel, plan, factor),
            out_shape=tuple(halves),
            in_specs=vmem(4),
            out_specs=tuple(vmem(2 * PARTS)),
            compiler_params=PARAMS,
            name="gradient",
        )(own, other, wanted, activations)
        summed = all_sum(plan, list(zip(pieces[::2], pieces[1::2])))
        square = pl.pallas_call(
            functools.partial(square_kernel, plan),
            out_shape=tile,
            in_specs=vmem(2 * PARTS),
            out_specs=vmem(1)[0],
            compiler_params=PARAMS,
            name="square",
        )(*summed)
        own, other = across_features(square)
        if iteration + 1 < ITERS:
            weights, ahead, product = pl.pallas_call(
                functools.partial(update_kernel, plan, momentum[iteration], False),
                out_shape=(state, state, small),
                in_specs=vmem(2 + 2 * PARTS + 3),
                out_specs=tuple(vmem(3)),
                compiler_params=PARAMS,
                name="update",
            )(own, other, *summed, weights, ahead, activations)
        else:
            weights = pl.pallas_call(
                functools.partial(update_kernel, plan, momentum[iteration], True),
                out_shape=state,
                in_specs=smem + vmem(2 + 2 * PARTS + 2),
                out_specs=vmem(1)[0],
                compiler_params=PARAMS,
                name="last",
            )(mask, own, other, *summed, weights, ahead)
    return weights


def solution(mesh):
    in_specs = (P("tok", "feat"), P(None, "feat"), P("tok", None))
    out_specs = P(None, "feat")
    return jax.shard_map(shards, mesh=mesh, in_specs=in_specs, out_specs=out_specs, check_vma=False)
```

```python
import functools
import math

import jax
import jax.numpy as jnp
from jax import lax
from jax.experimental import pallas as pl
from jax.experimental.pallas import tpu as pltpu
from jax.sharding import PartitionSpec as P

ITERS = 4
STEP = 0.25
THRESHOLD = 0.2
EPSILON = 1e-06
GROUP = 8
SHARES = (20, 19, 17)
PARTS = len(SHARES)
LANES = 128
VMEM_BYTES = 4 * 1024 * 1024

f32 = jnp.float32
bf16 = jnp.bfloat16


def momentum_terms(iterations):
    values = []
    current = 1.0
    for _ in range(iterations):
        upcoming = (1.0 + math.sqrt(1.0 + 4.0 * current * current)) / 2.0
        values.append((current - 1.0) / upcoming)
        current = upcoming
    return values


def swap(x, axis, bit):
    pairs = [(i, i ^ (1 << bit)) for i in range(lax.axis_size(axis))]
    return lax.ppermute(x, axis, pairs)


def bits_of(axis):
    return lax.axis_size(axis).bit_length() - 1


class Plan:
    def __init__(self, rows, columns, tokens):
        self.rows = rows
        self.columns = columns
        self.tokens = tokens
        self.rows_bits = min(bits_of("tok"), (rows // GROUP).bit_length() - 1)
        self.places = 1 << self.rows_bits
        self.height = rows >> self.rows_bits
        self.unit = next(u for u in (256, 128) if columns % u == 0)
        units = columns // self.unit
        self.entries = rows * columns * lax.axis_size("feat")
        self.factor = (columns * lax.axis_size("feat")) ** (-0.5)
        marks = [0]
        for share in SHARES:
            marks.append(marks[-1] + share)
        edges = [self.unit * round(units * m / marks[-1]) for m in marks]
        self.spans = list(zip(edges[:-1], edges[1:]))
        self.widths = [b - a for a, b in self.spans]
        self.orders = [[(p + s) % self.rows_bits for s in range(self.rows_bits)] for p in range(PARTS)]

    def blocks(self, p):
        a, b = self.spans[p]
        return [(slice(x - a, x - a + self.unit), slice(x, x + self.unit)) for x in range(a, b, self.unit)]

    def bit_value(self, level):
        return self.places >> (level + 1)

    def arrangement(self, p):
        result = [0]
        for level in reversed(self.orders[p]):
            result = result + [g + self.bit_value(level) for g in result]
        return result

    def mask(self):
        index = lax.axis_index("tok")
        return sum(((index >> level) & 1) * self.bit_value(level) for level in range(self.rows_bits))

    def rearranged(self, x, places):
        h = self.height
        return jnp.concatenate([x[h * g : h * (g + 1)] for g in places], 0)

    def to_part(self, p, x):
        return self.rearranged(x, self.arrangement(p))

    def from_part(self, p, x):
        order = self.arrangement(p)
        return self.rearranged(x, [order.index(g) for g in range(self.places)])


def dot_nt(a, b):
    return lax.dot_general(a, b, (((1,), (1,)), ((), ())), preferred_element_type=f32)


VMEM = pl.BlockSpec(memory_space=pltpu.VMEM)
SMEM = pl.BlockSpec(memory_space=pltpu.SMEM)


def run(kernel, name, outs, specs, args):
    return pl.pallas_call(
        kernel,
        out_shape=tuple(jax.ShapeDtypeStruct(shape, dtype) for shape, dtype in outs),
        in_specs=list(specs),
        out_specs=(VMEM,) * len(outs),
        compiler_params=pltpu.CompilerParams(vmem_limit_bytes=VMEM_BYTES),
        name=name,
    )(*args)


def first_kernel(plan, mask_ref, dense_ref, act_ref, *refs):
    *start_refs, product_ref = refs
    h = plan.height
    total = jnp.zeros(product_ref.shape, f32)
    for p, (a, b) in enumerate(plan.spans):
        for start in range(a, b, plan.unit):
            groups = []
            for g in range(plan.places):
                rows = pl.ds(pl.multiple_of((g ^ mask_ref[0]) * h, h), h)
                groups.append(dense_ref[rows, start : start + plan.unit])
            block = jnp.concatenate(groups, 0)
            start_refs[p][:, start - a : start - a + plan.unit] = block
            total = total + dot_nt(block.astype(bf16), act_ref[:, start : start + plan.unit])
    product_ref[...] = total


def gradient_kernel(plan, p, own_ref, other_ref, wanted_ref, act_ref, keep_ref, send_ref):
    residual = plan.factor * (own_ref[...] + other_ref[...]) - wanted_ref[...]
    half = plan.rows // 2
    arranged = plan.to_part(p, residual).astype(bf16)

    for here, there in plan.blocks(p):
        block = jnp.dot(arranged, act_ref[:, there], preferred_element_type=f32)
        keep_ref[:, here] = block[:half]
        send_ref[:, here] = block[half:].astype(bf16)


def pair_tile(value, rows):
    value = jnp.broadcast_to(value, (rows, LANES))
    high = value.astype(bf16).astype(f32)
    lane = lax.broadcasted_iota(jnp.int32, (rows, LANES), 1)
    return jnp.where(lane < LANES // 2, high, value - high).astype(bf16)


def pair_value(tile):
    tile = tile.astype(f32)
    return jnp.sum(tile, keepdims=True) / (tile.shape[0] * (LANES // 2))


def combine_kernel(plan, low_ref, came_ref, *outs):
    h = plan.height
    total = jnp.zeros((h, LANES), f32)
    for p, (a, b) in enumerate(plan.spans):
        for start in range(a, b, plan.unit):
            block = low_ref[:, start : start + plan.unit].astype(f32) + came_ref[:, start : start + plan.unit].astype(f32)
            block = block.astype(bf16)
            outs[p][:, start - a : start - a + plan.unit] = block
            block = block.astype(f32)
            for lane in range(0, plan.unit, LANES):
                piece = block[:, lane : lane + LANES]
                total = total + piece * piece
    outs[0][:, plan.widths[0] :] = pair_tile(jnp.sum(total, keepdims=True), h)


def join_kernel(plan, own_ref, came_ref, out_ref):
    h, width = own_ref.shape
    last = width - LANES
    for start in range(0, last, plan.unit):
        here = slice(start, start + plan.unit)
        out_ref[:, here] = jnp.concatenate([own_ref[:, here].astype(f32), came_ref[:, here].astype(f32)], 0).astype(bf16)
    square = pair_value(own_ref[:, last:]) + pair_value(came_ref[:, last:])
    out_ref[:, last:] = pair_tile(square, 2 * h)


def scale_of(plan, own_ref, other_ref):
    mean_square = pair_value(own_ref[...] + other_ref[...]) / plan.entries
    return STEP * lax.rsqrt(mean_square + EPSILON)


def shrink(plan, p, scale, kept_ref, came_ref, ahead_ref, here):
    gradient = jnp.concatenate([kept_ref[:, here].astype(f32), came_ref[:, here].astype(f32)], 0)
    moved = ahead_ref[:, here] - scale * plan.from_part(p, gradient)
    return moved - jnp.clip(moved, -THRESHOLD, THRESHOLD)


def update_kernel(plan, p, momentum, *refs):
    own_ref, other_ref, kept_ref, came_ref, weights_ref, ahead_ref, act_ref, *refs = refs
    *before, new_weights_ref, new_ahead_ref, product_ref = refs
    scale = scale_of(plan, own_ref, other_ref)
    total = before[0][...] if before else jnp.zeros(product_ref.shape, f32)

    for here, there in plan.blocks(p):
        shrunk = shrink(plan, p, scale, kept_ref, came_ref, ahead_ref, here)
        ahead = shrunk + momentum * (shrunk - weights_ref[:, here])
        new_weights_ref[:, here] = shrunk
        new_ahead_ref[:, here] = ahead
        total = total + dot_nt(ahead.astype(bf16), act_ref[:, there])
    product_ref[...] = total


def last_kernel(plan, mask_ref, own_ref, other_ref, *refs):
    *refs, out_ref = refs
    scale = scale_of(plan, own_ref, other_ref)
    h = plan.height
    for p in range(PARTS):
        kept_ref, came_ref, ahead_ref = refs[3 * p : 3 * p + 3]
        for here, there in plan.blocks(p):
            shrunk = shrink(plan, p, scale, kept_ref, came_ref, ahead_ref, here)
            for g in range(plan.places):
                rows = pl.ds(pl.multiple_of((g ^ mask_ref[0]) * h, h), h)
                out_ref[rows, there] = shrunk[h * g : h * (g + 1)]


def after(x, earlier):
    return lax.optimization_barrier((x, *earlier))[0]


def all_sum(plan, pieces):
    current = [kept for kept, _ in pieces]
    sends = [sent for _, sent in pieces]
    for stage in range(plan.rows_bits):
        came = [swap(sends[p], "tok", plan.orders[p][stage]) for p in range(PARTS)]
        for p in range(PARTS):
            arrived = after(came[p], sends[:p]) if p else came[p]
            whole = current[p] + arrived.astype(f32)
            middle = whole.shape[0] // 2 if stage + 1 < plan.rows_bits else 0
            sends[p] = whole[middle:].astype(bf16)
            current[p] = whole[:middle]
    low = jnp.concatenate(sends, 1)
    came = jnp.zeros_like(low)
    for bit in range(plan.rows_bits, bits_of("tok")):
        if bit > plan.rows_bits:
            low = (low.astype(f32) + came.astype(f32)).astype(bf16)
        came = swap(low, "tok", bit)
    outs = [((plan.height, width + (0 if p else LANES)), bf16) for p, width in enumerate(plan.widths)]
    current = run(functools.partial(combine_kernel, plan), "combine", outs, [VMEM] * 2, (low, came))
    current = list(current)
    for stage in reversed(range(plan.rows_bits)):
        came = [swap(current[p], "tok", plan.orders[p][stage]) for p in range(PARTS)]
        if stage:
            for p in range(PARTS):
                rows, width = current[p].shape
                arrived = after(came[p], current[:p]) if p else came[p]
                if p:
                    current[p] = jnp.concatenate([current[p], arrived], 0)
                else:
                    (current[p],) = run(
                        functools.partial(join_kernel, plan), "join", [((2 * rows, width), bf16)], [VMEM] * 2, (current[p], arrived)
                    )
    return list(zip(current, came))


def across_features(x):
    count = bits_of("feat")
    for bit in range(count - 1):
        x = x + swap(x, "feat", bit)
    return x, swap(x, "feat", count - 1)


def shards(activations, dense_rows, targets):
    rows, columns = dense_rows.shape
    tokens = activations.shape[0]
    plan = Plan(rows, columns, tokens)
    momentum = momentum_terms(ITERS)
    wanted = targets.T
    for level in range(plan.rows_bits):
        cut = wanted.reshape(-1, 2, rows >> (level + 1), tokens)
        bit = (lax.axis_index("tok") >> level) & 1
        wanted = jnp.where(bit == 1, cut[:, ::-1], cut).reshape(rows, tokens)
    mask = plan.mask().reshape(1).astype(jnp.int32)
    states = [((rows, width), f32) for width in plan.widths]
    small = ((rows, tokens), f32)

    *ahead, product = run(
        functools.partial(first_kernel, plan),
        "first",
        states + [small],
        [SMEM, VMEM, VMEM],
        (mask, dense_rows, activations),
    )
    weights = list(ahead)
    for iteration in range(ITERS):
        own, other = across_features(product)
        pieces = [
            run(
                functools.partial(gradient_kernel, plan, p),
                "gradient",
                [((rows // 2, plan.widths[p]), f32), ((rows // 2, plan.widths[p]), bf16)],
                [VMEM] * 4,
                (own, other, wanted, activations),
            )
            for p in range(PARTS)
        ]
        halves = all_sum(plan, pieces)
        kept, came = halves[0]
        last = plan.widths[0]
        own, other = across_features(kept[:8, last:].astype(f32) + came[:8, last:].astype(f32))
        if iteration + 1 < ITERS:
            before = ()
            for p in range(PARTS):
                weights[p], ahead[p], product = run(
                    functools.partial(update_kernel, plan, p, momentum[iteration]),
                    "update",
                    [states[p], states[p], small],
                    [VMEM] * (7 + len(before)),
                    (own, other, *halves[p], weights[p], ahead[p], activations, *before),
                )
                before = (product,)
        else:
            args = [x for p in range(PARTS) for x in (*halves[p], ahead[p])]
            (result,) = run(
                functools.partial(last_kernel, plan),
                "last",
                [((rows, columns), f32)],
                [SMEM] + [VMEM] * (2 + len(args)),
                (mask, own, other, *args),
            )
    return result


def solution(mesh):
    in_specs = (P("tok", "feat"), P(None, "feat"), P("tok", None))
    out_specs = P(None, "feat")
    return jax.shard_map(shards, mesh=mesh, in_specs=in_specs, out_specs=out_specs, check_vma=False)
```

```python
import functools
import math

import jax
import jax.numpy as jnp
from jax import lax
from jax.experimental import pallas as pl
from jax.experimental.pallas import tpu as pltpu
from jax.sharding import PartitionSpec as P

ITERS = 4
STEP = 0.25
THRESHOLD = 0.2
EPSILON = 1e-06
GROUP = 8
SHARES = (20, 19, 17)
PARTS = len(SHARES)
LANES = 128
VMEM_BYTES = 4 * 1024 * 1024

f32 = jnp.float32
bf16 = jnp.bfloat16


def momentum_terms(iterations):
    values = []
    current = 1.0
    for _ in range(iterations):
        upcoming = (1.0 + math.sqrt(1.0 + 4.0 * current * current)) / 2.0
        values.append((current - 1.0) / upcoming)
        current = upcoming
    return values


def swap(x, axis, bit):
    pairs = [(i, i ^ (1 << bit)) for i in range(lax.axis_size(axis))]
    return lax.ppermute(x, axis, pairs)


def bits_of(axis):
    return lax.axis_size(axis).bit_length() - 1


class Plan:
    def __init__(self, rows, columns, tokens):
        self.rows = rows
        self.columns = columns
        self.tokens = tokens
        self.rows_bits = min(bits_of("tok"), (rows // GROUP).bit_length() - 1)
        self.places = 1 << self.rows_bits
        self.height = rows >> self.rows_bits
        self.unit = next(u for u in (256, 128) if columns % u == 0)
        units = columns // self.unit
        self.entries = rows * columns * lax.axis_size("feat")
        self.factor = (columns * lax.axis_size("feat")) ** (-0.5)
        marks = [0]
        for share in SHARES:
            marks.append(marks[-1] + share)
        edges = [self.unit * round(units * m / marks[-1]) for m in marks]
        self.spans = list(zip(edges[:-1], edges[1:]))
        self.widths = [b - a for a, b in self.spans]
        self.orders = [[(p + s) % self.rows_bits for s in range(self.rows_bits)] for p in range(PARTS)]

    def blocks(self, p):
        a, b = self.spans[p]
        return [(slice(x - a, x - a + self.unit), slice(x, x + self.unit)) for x in range(a, b, self.unit)]

    def bit_value(self, level):
        return self.places >> (level + 1)

    def arrangement(self, p):
        result = [0]
        for level in reversed(self.orders[p]):
            result = result + [g + self.bit_value(level) for g in result]
        return result

    def mask(self):
        index = lax.axis_index("tok")
        return sum(((index >> level) & 1) * self.bit_value(level) for level in range(self.rows_bits))

    def rearranged(self, x, places):
        h = self.height
        return jnp.concatenate([x[h * g : h * (g + 1)] for g in places], 0)

    def to_part(self, p, x):
        return self.rearranged(x, self.arrangement(p))

    def from_part(self, p, x):
        order = self.arrangement(p)
        return self.rearranged(x, [order.index(g) for g in range(self.places)])


def dot_nt(a, b):
    return lax.dot_general(a, b, (((1,), (1,)), ((), ())), preferred_element_type=f32)


VMEM = pl.BlockSpec(memory_space=pltpu.VMEM)
SMEM = pl.BlockSpec(memory_space=pltpu.SMEM)


def run(kernel, name, outs, specs, args):
    return pl.pallas_call(
        kernel,
        out_shape=tuple(jax.ShapeDtypeStruct(shape, dtype) for shape, dtype in outs),
        in_specs=list(specs),
        out_specs=(VMEM,) * len(outs),
        compiler_params=pltpu.CompilerParams(vmem_limit_bytes=VMEM_BYTES),
        name=name,
    )(*args)


def first_kernel(plan, mask_ref, dense_ref, targets_ref, act_ref, *refs):
    *start_refs, wanted_ref, product_ref = refs
    h = plan.height
    for g in range(plan.places):
        rows = pl.ds(pl.multiple_of((g ^ mask_ref[0]) * h, h), h)
        wanted_ref[g * h : (g + 1) * h] = targets_ref[rows, :]
    total = jnp.zeros(product_ref.shape, f32)
    for p, (a, b) in enumerate(plan.spans):
        for start in range(a, b, plan.unit):
            groups = []
            for g in range(plan.places):
                rows = pl.ds(pl.multiple_of((g ^ mask_ref[0]) * h, h), h)
                groups.append(dense_ref[rows, start : start + plan.unit])
            block = jnp.concatenate(groups, 0)
            start_refs[p][:, start - a : start - a + plan.unit] = block
            total = total + dot_nt(block.astype(bf16), act_ref[:, start : start + plan.unit])
    product_ref[...] = total


def gradient_kernel(plan, p, own_ref, other_ref, wanted_ref, act_ref, keep_ref, send_ref):
    residual = plan.factor * (own_ref[...] + other_ref[...]) - wanted_ref[...]
    half = plan.rows // 2
    arranged = plan.to_part(p, residual).astype(bf16)

    for here, there in plan.blocks(p):
        block = jnp.dot(arranged, act_ref[:, there], preferred_element_type=f32)
        keep_ref[:, here] = block[:half]
        send_ref[:, here] = block[half:].astype(bf16)


def pair_tile(value, rows):
    value = jnp.broadcast_to(value, (rows, LANES))
    high = value.astype(bf16).astype(f32)
    lane = lax.broadcasted_iota(jnp.int32, (rows, LANES), 1)
    return jnp.where(lane < LANES // 2, high, value - high).astype(bf16)


def pair_value(tile):
    tile = tile.astype(f32)
    return jnp.sum(tile, keepdims=True) / (tile.shape[0] * (LANES // 2))


def combine_kernel(plan, p, low_ref, came_ref, *refs):
    total = refs[0][...] if p else jnp.zeros((plan.height, LANES), f32)
    out_ref = refs[1] if p else refs[0]
    for here, _ in plan.blocks(p):
        block = (low_ref[:, here].astype(f32) + came_ref[:, here].astype(f32)).astype(bf16)
        out_ref[:, here] = block
        block = block.astype(f32)
        for lane in range(0, plan.unit, LANES):
            piece = block[:, lane : lane + LANES]
            total = total + piece * piece
    if p + 1 < PARTS:
        refs[-1][...] = total
    else:
        out_ref[:, plan.widths[p] :] = pair_tile(jnp.sum(total, keepdims=True), plan.height)


def join_kernel(plan, own_ref, came_ref, out_ref):
    h, width = own_ref.shape
    last = width - LANES
    for start in range(0, last, plan.unit):
        here = slice(start, start + plan.unit)
        out_ref[:, here] = jnp.concatenate([own_ref[:, here].astype(f32), came_ref[:, here].astype(f32)], 0).astype(bf16)
    square = pair_value(own_ref[:, last:]) + pair_value(came_ref[:, last:])
    out_ref[:, last:] = pair_tile(square, 2 * h)


def scale_of(plan, own_ref, other_ref):
    mean_square = pair_value(own_ref[...] + other_ref[...]) / plan.entries
    return STEP * lax.rsqrt(mean_square + EPSILON)


def shrink(plan, p, scale, kept_ref, came_ref, ahead_ref, here):
    gradient = jnp.concatenate([kept_ref[:, here].astype(f32), came_ref[:, here].astype(f32)], 0)
    moved = ahead_ref[:, here] - scale * plan.from_part(p, gradient)
    return moved - jnp.clip(moved, -THRESHOLD, THRESHOLD)


def update_kernel(plan, p, momentum, *refs):
    own_ref, other_ref, kept_ref, came_ref, weights_ref, ahead_ref, act_ref, *refs = refs
    *before, new_weights_ref, new_ahead_ref, product_ref = refs
    scale = scale_of(plan, own_ref, other_ref)
    total = before[0][...] if before else jnp.zeros(product_ref.shape, f32)

    for here, there in plan.blocks(p):
        shrunk = shrink(plan, p, scale, kept_ref, came_ref, ahead_ref, here)
        ahead = shrunk + momentum * (shrunk - weights_ref[:, here])
        new_weights_ref[:, here] = shrunk
        new_ahead_ref[:, here] = ahead
        total = total + dot_nt(ahead.astype(bf16), act_ref[:, there])
    product_ref[...] = total


def last_kernel(plan, mask_ref, own_ref, other_ref, *refs):
    *refs, out_ref = refs
    scale = scale_of(plan, own_ref, other_ref)
    h = plan.height
    for p in range(PARTS):
        kept_ref, came_ref, ahead_ref = refs[3 * p : 3 * p + 3]
        for here, there in plan.blocks(p):
            shrunk = shrink(plan, p, scale, kept_ref, came_ref, ahead_ref, here)
            for g in range(plan.places):
                rows = pl.ds(pl.multiple_of((g ^ mask_ref[0]) * h, h), h)
                out_ref[rows, there] = shrunk[h * g : h * (g + 1)]


def after(x, earlier):
    return lax.optimization_barrier((x, *earlier))[0]


def all_sum(plan, pieces):
    current = [kept for kept, _ in pieces]
    sends = [sent for _, sent in pieces]
    for stage in range(plan.rows_bits):
        came = [swap(sends[p], "tok", plan.orders[p][stage]) for p in range(PARTS)]
        for p in range(PARTS):
            arrived = after(came[p], sends[:p]) if p else came[p]
            whole = current[p] + arrived.astype(f32)
            middle = whole.shape[0] // 2 if stage + 1 < plan.rows_bits else 0
            sends[p] = whole[middle:].astype(bf16)
            current[p] = whole[:middle]
    came = [None] * PARTS
    for bit in range(plan.rows_bits, bits_of("tok")):
        if bit > plan.rows_bits:
            sends = [(a.astype(f32) + b.astype(f32)).astype(bf16) for a, b in zip(sends, came)]
        came = [swap(x, "tok", bit) for x in sends]
    square = ()
    for p, width in enumerate(plan.widths):
        last = p + 1 == PARTS
        outs = [((plan.height, width + LANES * last), bf16)] + [((plan.height, LANES), f32)] * (not last)
        current[p], *square = run(
            functools.partial(combine_kernel, plan, p), "combine", outs, [VMEM] * (2 + len(square)), (sends[p], came[p], *square)
        )
    for stage in reversed(range(plan.rows_bits)):
        came = [swap(current[p], "tok", plan.orders[p][stage]) for p in range(PARTS)]
        if stage:
            for p in range(PARTS):
                rows, width = current[p].shape
                arrived = after(came[p], current[:p]) if p else came[p]
                if p + 1 < PARTS:
                    current[p] = jnp.concatenate([current[p], arrived], 0)
                else:
                    (current[p],) = run(
                        functools.partial(join_kernel, plan), "join", [((2 * rows, width), bf16)], [VMEM] * 2, (current[p], arrived)
                    )
    return list(zip(current, came))


def across_features(x):
    count = bits_of("feat")
    for bit in range(count - 1):
        x = x + swap(x, "feat", bit)
    return x, swap(x, "feat", count - 1)


def shards(activations, dense_rows, targets):
    rows, columns = dense_rows.shape
    tokens = activations.shape[0]
    plan = Plan(rows, columns, tokens)
    momentum = momentum_terms(ITERS)
    mask = plan.mask().reshape(1).astype(jnp.int32)
    states = [((rows, width), f32) for width in plan.widths]
    small = ((rows, tokens), f32)

    *ahead, wanted, product = run(
        functools.partial(first_kernel, plan),
        "first",
        states + [small, small],
        [SMEM, VMEM, VMEM, VMEM],
        (mask, dense_rows, targets.T, activations),
    )
    weights = list(ahead)
    for iteration in range(ITERS):
        own, other = across_features(product)
        pieces = [
            run(
                functools.partial(gradient_kernel, plan, p),
                "gradient",
                [((rows // 2, plan.widths[p]), f32), ((rows // 2, plan.widths[p]), bf16)],
                [VMEM] * 4,
                (own, other, wanted, activations),
            )
            for p in range(PARTS)
        ]
        halves = all_sum(plan, pieces)
        kept, came = halves[-1]
        last = plan.widths[-1]
        own, other = across_features(kept[:8, last:].astype(f32) + came[:8, last:].astype(f32))
        if iteration + 1 < ITERS:
            before = ()
            for p in range(PARTS):
                weights[p], ahead[p], product = run(
                    functools.partial(update_kernel, plan, p, momentum[iteration]),
                    "update",
                    [states[p], states[p], small],
                    [VMEM] * (7 + len(before)),
                    (own, other, *halves[p], weights[p], ahead[p], activations, *before),
                )
                before = (product,)
        else:
            args = [x for p in range(PARTS) for x in (*halves[p], ahead[p])]
            (result,) = run(
                functools.partial(last_kernel, plan),
                "last",
                [((rows, columns), f32)],
                [SMEM] + [VMEM] * (2 + len(args)),
                (mask, own, other, *args),
            )
    return result


def solution(mesh):
    in_specs = (P("tok", "feat"), P(None, "feat"), P("tok", None))
    out_specs = P(None, "feat")
    return jax.shard_map(shards, mesh=mesh, in_specs=in_specs, out_specs=out_specs, check_vma=False)
```

```python
import functools
import math

import jax
import jax.numpy as jnp
from jax import lax
from jax.experimental import pallas as pl
from jax.experimental.pallas import tpu as pltpu
from jax.sharding import PartitionSpec as P

ITERS = 4
STEP = 0.25
THRESHOLD = 0.2
EPSILON = 1e-06
GROUP = 8
SHARES = (16, 16, 16, 8)
PARTS = len(SHARES)
LANES = 128
VMEM_BYTES = 4 * 1024 * 1024

f32 = jnp.float32
bf16 = jnp.bfloat16


def momentum_terms(iterations):
    values = []
    current = 1.0
    for _ in range(iterations):
        upcoming = (1.0 + math.sqrt(1.0 + 4.0 * current * current)) / 2.0
        values.append((current - 1.0) / upcoming)
        current = upcoming
    return values


def swap(x, axis, bit):
    pairs = [(i, i ^ (1 << bit)) for i in range(lax.axis_size(axis))]
    return lax.ppermute(x, axis, pairs)


def bits_of(axis):
    return lax.axis_size(axis).bit_length() - 1


class Plan:
    def __init__(self, rows, columns, tokens):
        self.rows = rows
        self.columns = columns
        self.tokens = tokens
        self.rows_bits = min(bits_of("tok"), (rows // GROUP).bit_length() - 1)
        self.places = 1 << self.rows_bits
        self.height = rows >> self.rows_bits
        self.unit = next(u for u in (256, 128) if columns % u == 0)
        units = columns // self.unit
        self.entries = rows * columns * lax.axis_size("feat")
        self.factor = (columns * lax.axis_size("feat")) ** (-0.5)
        marks = [0]
        for share in SHARES:
            marks.append(marks[-1] + share)
        edges = [self.unit * round(units * m / marks[-1]) for m in marks]
        self.spans = list(zip(edges[:-1], edges[1:]))
        self.widths = [b - a for a, b in self.spans]
        levels = range(self.rows_bits)
        self.scatter = [[(p + s) % self.rows_bits for s in levels] for p in range(PARTS)]
        self.gather = [[(p + s) % self.rows_bits for s in levels] for p in range(PARTS)]

    def blocks(self, p):
        a, b = self.spans[p]
        return [(slice(x - a, x - a + self.unit), slice(x, x + self.unit)) for x in range(a, b, self.unit)]

    def bit_value(self, level):
        return self.places >> (level + 1)

    def arrangement(self, levels):
        result = [0]
        for level in levels:
            result = result + [g + self.bit_value(level) for g in result]
        return result

    def mask(self):
        index = lax.axis_index("tok")
        return sum(((index >> level) & 1) * self.bit_value(level) for level in range(self.rows_bits))

    def rearranged(self, x, places):
        h = self.height
        return jnp.concatenate([x[h * g : h * (g + 1)] for g in places], 0)

    def to_part(self, p, x):
        return self.rearranged(x, self.arrangement(self.scatter[p][::-1]))

    def from_part(self, p, x):
        order = self.arrangement(self.gather[p])
        return self.rearranged(x, [order.index(g) for g in range(self.places)])


def dot_nt(a, b):
    return lax.dot_general(a, b, (((1,), (1,)), ((), ())), preferred_element_type=f32)


VMEM = pl.BlockSpec(memory_space=pltpu.VMEM)
SMEM = pl.BlockSpec(memory_space=pltpu.SMEM)


def run(kernel, name, outs, specs, args):
    return pl.pallas_call(
        kernel,
        out_shape=tuple(jax.ShapeDtypeStruct(shape, dtype) for shape, dtype in outs),
        in_specs=list(specs),
        out_specs=(VMEM,) * len(outs),
        compiler_params=pltpu.CompilerParams(vmem_limit_bytes=VMEM_BYTES),
        name=name,
    )(*args)


def order_kernel(plan, mask_ref, targets_ref, wanted_ref):
    h = plan.height
    for g in range(plan.places):
        rows = pl.ds(pl.multiple_of((g ^ mask_ref[0]) * h, h), h)
        wanted_ref[g * h : (g + 1) * h] = targets_ref[rows, :]


def start_kernel(plan, mask_ref, dense_ref, *start_refs):
    h = plan.height
    for p in range(PARTS):
        for g in range(plan.places):
            rows = pl.ds(pl.multiple_of((g ^ mask_ref[0]) * h, h), h)
            for here, there in plan.blocks(p):
                start_refs[p][g * h : (g + 1) * h, here] = dense_ref[rows, there]


def first_kernel(plan, *refs):
    *start_refs, act_ref, product_ref = refs
    total = jnp.zeros(product_ref.shape, f32)
    for p in range(PARTS):
        for here, there in plan.blocks(p):
            total = total + dot_nt(start_refs[p][:, here].astype(bf16), act_ref[:, there])
    product_ref[...] = total


def gradient_kernel(plan, p, own_ref, other_ref, wanted_ref, act_ref, keep_ref, send_ref):
    residual = plan.factor * (own_ref[...] + other_ref[...]) - wanted_ref[...]
    half = plan.rows // 2
    arranged = plan.to_part(p, residual).astype(bf16)

    for here, there in plan.blocks(p):
        block = jnp.dot(arranged, act_ref[:, there], preferred_element_type=f32)
        keep_ref[:, here] = block[:half]
        send_ref[:, here] = block[half:].astype(bf16)


def pair_tile(value, rows):
    value = jnp.broadcast_to(value, (rows, LANES))
    high = value.astype(bf16).astype(f32)
    lane = lax.broadcasted_iota(jnp.int32, (rows, LANES), 1)
    return jnp.where(lane < LANES // 2, high, value - high).astype(bf16)


def pair_value(tile):
    tile = tile.astype(f32)
    return jnp.sum(tile, keepdims=True) / (tile.shape[0] * (LANES // 2))


def combine_kernel(plan, p, low_ref, came_ref, *refs):
    total = refs[0][...] if p else jnp.zeros((plan.height, LANES), f32)
    out_ref = refs[1] if p else refs[0]
    for here, _ in plan.blocks(p):
        block = (low_ref[:, here].astype(f32) + came_ref[:, here].astype(f32)).astype(bf16)
        out_ref[:, here] = block
        block = block.astype(f32)
        for lane in range(0, plan.unit, LANES):
            piece = block[:, lane : lane + LANES]
            total = total + piece * piece
    if p + 1 < PARTS:
        refs[-1][...] = total
    else:
        out_ref[:, plan.widths[p] :] = pair_tile(jnp.sum(total, keepdims=True), plan.height)


def join_kernel(plan, own_ref, came_ref, out_ref):
    h, width = own_ref.shape
    last = width - LANES
    for start in range(0, last, plan.unit):
        here = slice(start, start + plan.unit)
        out_ref[:, here] = jnp.concatenate([own_ref[:, here].astype(f32), came_ref[:, here].astype(f32)], 0).astype(bf16)
    square = pair_value(own_ref[:, last:]) + pair_value(came_ref[:, last:])
    out_ref[:, last:] = pair_tile(square, 2 * h)


def scale_of(plan, own_ref, other_ref):
    mean_square = pair_value(own_ref[...] + other_ref[...]) / plan.entries
    return STEP * lax.rsqrt(mean_square + EPSILON)


def shrink(plan, p, scale, kept_ref, came_ref, ahead_ref, here):
    gradient = jnp.concatenate([kept_ref[:, here].astype(f32), came_ref[:, here].astype(f32)], 0)
    moved = ahead_ref[:, here] - scale * plan.from_part(p, gradient)
    return moved - jnp.clip(moved, -THRESHOLD, THRESHOLD)


def update_kernel(plan, p, momentum, *refs):
    own_ref, other_ref, kept_ref, came_ref, weights_ref, ahead_ref, act_ref, *refs = refs
    *before, new_weights_ref, new_ahead_ref, product_ref = refs
    scale = scale_of(plan, own_ref, other_ref)
    total = before[0][...] if before else jnp.zeros(product_ref.shape, f32)

    for here, there in plan.blocks(p):
        shrunk = shrink(plan, p, scale, kept_ref, came_ref, ahead_ref, here)
        ahead = shrunk + momentum * (shrunk - weights_ref[:, here])
        new_weights_ref[:, here] = shrunk
        new_ahead_ref[:, here] = ahead
        total = total + dot_nt(ahead.astype(bf16), act_ref[:, there])
    product_ref[...] = total


def last_kernel(plan, mask_ref, own_ref, other_ref, *refs):
    *refs, out_ref = refs
    scale = scale_of(plan, own_ref, other_ref)
    h = plan.height
    for p in range(PARTS):
        kept_ref, came_ref, ahead_ref = refs[3 * p : 3 * p + 3]
        for here, there in plan.blocks(p):
            shrunk = shrink(plan, p, scale, kept_ref, came_ref, ahead_ref, here)
            for g in range(plan.places):
                rows = pl.ds(pl.multiple_of((g ^ mask_ref[0]) * h, h), h)
                out_ref[rows, there] = shrunk[h * g : h * (g + 1)]


def after(x, earlier):
    return lax.optimization_barrier((x, *earlier))[0]


def all_sum(plan, pieces):
    current = [kept for kept, _ in pieces]
    sends = [sent for _, sent in pieces]
    for stage in range(plan.rows_bits):
        came = [swap(sends[p], "tok", plan.scatter[p][stage]) for p in range(PARTS)]
        for p in range(PARTS):
            arrived = after(came[p], sends[:p]) if p else came[p]
            whole = current[p] + arrived.astype(f32)
            middle = whole.shape[0] // 2 if stage + 1 < plan.rows_bits else 0
            sends[p] = whole[middle:].astype(bf16)
            current[p] = whole[:middle]
    came = [None] * PARTS
    for bit in range(plan.rows_bits, bits_of("tok")):
        if bit > plan.rows_bits:
            sends = [(a.astype(f32) + b.astype(f32)).astype(bf16) for a, b in zip(sends, came)]
        came = [swap(x, "tok", bit) for x in sends]
    square = ()
    for p, width in enumerate(plan.widths):
        last = p + 1 == PARTS
        outs = [((plan.height, width + LANES * last), bf16)] + [((plan.height, LANES), f32)] * (not last)
        current[p], *square = run(
            functools.partial(combine_kernel, plan, p), "combine", outs, [VMEM] * (2 + len(square)), (sends[p], came[p], *square)
        )
    for stage in range(plan.rows_bits):
        came = [swap(current[p], "tok", plan.gather[p][stage]) for p in range(PARTS)]
        if stage + 1 < plan.rows_bits:
            for p in range(PARTS):
                rows, width = current[p].shape
                arrived = after(came[p], current[:p]) if p else came[p]
                if p + 1 < PARTS:
                    current[p] = jnp.concatenate([current[p], arrived], 0)
                else:
                    (current[p],) = run(
                        functools.partial(join_kernel, plan), "join", [((2 * rows, width), bf16)], [VMEM] * 2, (current[p], arrived)
                    )
    return list(zip(current, came))


def across_features(x):
    count = bits_of("feat")
    for bit in range(count - 1):
        x = x + swap(x, "feat", bit)
    return x, swap(x, "feat", count - 1)


def shards(activations, dense_rows, targets):
    rows, columns = dense_rows.shape
    tokens = activations.shape[0]
    plan = Plan(rows, columns, tokens)
    momentum = momentum_terms(ITERS)
    mask = plan.mask().reshape(1).astype(jnp.int32)
    states = [((rows, width), f32) for width in plan.widths]
    small = ((rows, tokens), f32)

    ahead = run(functools.partial(start_kernel, plan), "start", states, [SMEM, VMEM], (mask, dense_rows))
    ahead = list(ahead)
    (product,) = run(
        functools.partial(first_kernel, plan), "first", [small], [VMEM] * (PARTS + 1), (*ahead, activations)
    )
    (wanted,) = run(functools.partial(order_kernel, plan), "order", [small], [SMEM, VMEM], (mask, targets.T))
    weights = list(ahead)
    for iteration in range(ITERS):
        own, other = across_features(product)
        pieces = [
            run(
                functools.partial(gradient_kernel, plan, p),
                "gradient",
                [((rows // 2, plan.widths[p]), f32), ((rows // 2, plan.widths[p]), bf16)],
                [VMEM] * 4,
                (own, other, wanted, activations),
            )
            for p in range(PARTS)
        ]
        halves = all_sum(plan, pieces)
        kept, came = halves[-1]
        last = plan.widths[-1]
        own, other = across_features(kept[:8, last:].astype(f32) + came[:8, last:].astype(f32))
        if iteration + 1 < ITERS:
            before = ()
            for p in range(PARTS):
                weights[p], ahead[p], product = run(
                    functools.partial(update_kernel, plan, p, momentum[iteration]),
                    "update",
                    [states[p], states[p], small],
                    [VMEM] * (7 + len(before)),
                    (own, other, *halves[p], weights[p], ahead[p], activations, *before),
                )
                before = (product,)
        else:
            args = [x for p in range(PARTS) for x in (*halves[p], ahead[p])]
            (result,) = run(
                functools.partial(last_kernel, plan),
                "last",
                [((rows, columns), f32)],
                [SMEM] + [VMEM] * (2 + len(args)),
                (mask, own, other, *args),
            )
    return result


def solution(mesh):
    in_specs = (P("tok", "feat"), P(None, "feat"), P("tok", None))
    out_specs = P(None, "feat")
    return jax.shard_map(shards, mesh=mesh, in_specs=in_specs, out_specs=out_specs, check_vma=False)
```

```python
import functools
import math

import jax
import jax.numpy as jnp
from jax import lax
from jax.experimental import pallas as pl
from jax.experimental.pallas import tpu as pltpu
from jax.sharding import PartitionSpec as P

ITERS = 4
STEP = 0.25
THRESHOLD = 0.2
EPSILON = 1e-06
GROUP = 8
SHARES = (16, 16, 16, 8)
PARTS = len(SHARES)
LANES = 128
VMEM_BYTES = 4 * 1024 * 1024

f32 = jnp.float32
bf16 = jnp.bfloat16


def momentum_terms(iterations):
    values = []
    current = 1.0
    for _ in range(iterations):
        upcoming = (1.0 + math.sqrt(1.0 + 4.0 * current * current)) / 2.0
        values.append((current - 1.0) / upcoming)
        current = upcoming
    return values


def swap(x, axis, bit):
    pairs = [(i, i ^ (1 << bit)) for i in range(lax.axis_size(axis))]
    return lax.ppermute(x, axis, pairs)


def bits_of(axis):
    return lax.axis_size(axis).bit_length() - 1


class Plan:
    def __init__(self, rows, columns, tokens):
        self.rows = rows
        self.columns = columns
        self.tokens = tokens
        self.rows_bits = min(bits_of("tok"), (rows // GROUP).bit_length() - 1)
        self.places = 1 << self.rows_bits
        self.height = rows >> self.rows_bits
        self.unit = next(u for u in (256, 128) if columns % u == 0)
        units = columns // self.unit
        self.entries = rows * columns * lax.axis_size("feat")
        self.factor = (columns * lax.axis_size("feat")) ** (-0.5)
        marks = [0]
        for share in SHARES:
            marks.append(marks[-1] + share)
        edges = [self.unit * round(units * m / marks[-1]) for m in marks]
        self.spans = list(zip(edges[:-1], edges[1:]))
        self.widths = [b - a for a, b in self.spans]
        levels = range(self.rows_bits)
        self.scatter = [[(p + s) % self.rows_bits for s in levels] for p in range(PARTS)]
        self.gather = [[(p + s) % self.rows_bits for s in levels] for p in range(PARTS)]

    def blocks(self, p):
        a, b = self.spans[p]
        return [(slice(x - a, x - a + self.unit), slice(x, x + self.unit)) for x in range(a, b, self.unit)]

    def bit_value(self, level):
        return self.places >> (level + 1)

    def arrangement(self, levels):
        result = [0]
        for level in levels:
            result = result + [g + self.bit_value(level) for g in result]
        return result

    def mask(self):
        index = lax.axis_index("tok")
        return sum(((index >> level) & 1) * self.bit_value(level) for level in range(self.rows_bits))

    def rearranged(self, x, places):
        h = self.height
        return jnp.concatenate([x[h * g : h * (g + 1)] for g in places], 0)

    def to_part(self, p, x):
        return self.rearranged(x, self.arrangement(self.scatter[p][::-1]))

    def from_part(self, p, x):
        order = self.arrangement(self.gather[p])
        return self.rearranged(x, [order.index(g) for g in range(self.places)])


def dot_nt(a, b):
    return lax.dot_general(a, b, (((1,), (1,)), ((), ())), preferred_element_type=f32)


VMEM = pl.BlockSpec(memory_space=pltpu.VMEM)
HBM = pl.BlockSpec(memory_space=pltpu.HBM)
SMEM = pl.BlockSpec(memory_space=pltpu.SMEM)


def run(kernel, name, outs, specs, args, place=VMEM, scratch=(), limit=VMEM_BYTES):
    return pl.pallas_call(
        kernel,
        out_shape=tuple(jax.ShapeDtypeStruct(shape, dtype) for shape, dtype in outs),
        in_specs=list(specs),
        out_specs=(place,) * len(outs),
        scratch_shapes=list(scratch),
        compiler_params=pltpu.CompilerParams(vmem_limit_bytes=limit),
        name=name,
    )(*args)


def order_kernel(plan, mask_ref, targets_ref, wanted_ref):
    h = plan.height
    for g in range(plan.places):
        rows = pl.ds(pl.multiple_of((g ^ mask_ref[0]) * h, h), h)
        wanted_ref[g * h : (g + 1) * h] = targets_ref[rows, :]


def start_kernel(plan, mask_ref, dense_ref, *start_refs):
    h = plan.height
    for p in range(PARTS):
        for g in range(plan.places):
            rows = pl.ds(pl.multiple_of((g ^ mask_ref[0]) * h, h), h)
            for here, there in plan.blocks(p):
                start_refs[p][g * h : (g + 1) * h, here] = dense_ref[rows, there]


def first_kernel(plan, *refs):
    *start_refs, act_ref, product_ref = refs
    total = jnp.zeros(product_ref.shape, f32)
    for p in range(PARTS):
        for here, there in plan.blocks(p):
            total = total + dot_nt(start_refs[p][:, here].astype(bf16), act_ref[:, there])
    product_ref[...] = total


def gradient_kernel(plan, p, own_ref, other_ref, wanted_ref, act_ref, keep_ref, send_ref):
    residual = plan.factor * (own_ref[...] + other_ref[...]) - wanted_ref[...]
    half = plan.rows // 2
    arranged = plan.to_part(p, residual).astype(bf16)

    for here, there in plan.blocks(p):
        block = jnp.dot(arranged, act_ref[:, there], preferred_element_type=f32)
        keep_ref[:, here] = block[:half]
        send_ref[:, here] = block[half:].astype(bf16)


def pair_tile(value, rows):
    value = jnp.broadcast_to(value, (rows, LANES))
    high = value.astype(bf16).astype(f32)
    lane = lax.broadcasted_iota(jnp.int32, (rows, LANES), 1)
    return jnp.where(lane < LANES // 2, high, value - high).astype(bf16)


def pair_value(tile):
    tile = tile.astype(f32)
    return jnp.sum(tile, keepdims=True) / (tile.shape[0] * (LANES // 2))


def combine_kernel(plan, p, low_ref, came_ref, *refs):
    total = refs[0][...] if p else jnp.zeros((plan.height, LANES), f32)
    out_ref = refs[1] if p else refs[0]
    for here, _ in plan.blocks(p):
        block = (low_ref[:, here].astype(f32) + came_ref[:, here].astype(f32)).astype(bf16)
        out_ref[:, here] = block
        block = block.astype(f32)
        for lane in range(0, plan.unit, LANES):
            piece = block[:, lane : lane + LANES]
            total = total + piece * piece
    if p + 1 < PARTS:
        refs[-1][...] = total
    else:
        out_ref[:, plan.widths[p] :] = pair_tile(jnp.sum(total, keepdims=True), plan.height)


def join_kernel(plan, own_ref, came_ref, out_ref):
    h, width = own_ref.shape
    last = width - LANES
    for start in range(0, last, plan.unit):
        here = slice(start, start + plan.unit)
        out_ref[:, here] = jnp.concatenate([own_ref[:, here].astype(f32), came_ref[:, here].astype(f32)], 0).astype(bf16)
    square = pair_value(own_ref[:, last:]) + pair_value(came_ref[:, last:])
    out_ref[:, last:] = pair_tile(square, 2 * h)


def scale_of(plan, own_ref, other_ref):
    mean_square = pair_value(own_ref[...] + other_ref[...]) / plan.entries
    return STEP * lax.rsqrt(mean_square + EPSILON)


def shrink(plan, p, scale, kept_ref, came_ref, ahead_ref, here):
    gradient = jnp.concatenate([kept_ref[:, here].astype(f32), came_ref[:, here].astype(f32)], 0)
    moved = ahead_ref[:, here] - scale * plan.from_part(p, gradient)
    return moved - jnp.clip(moved, -THRESHOLD, THRESHOLD)


def update_kernel(plan, p, momentum, *refs):
    own_ref, other_ref, kept_ref, came_ref, weights_ref, ahead_ref, act_ref, *refs = refs
    *before, new_weights_ref, new_ahead_ref, product_ref = refs
    scale = scale_of(plan, own_ref, other_ref)
    total = before[0][...] if before else jnp.zeros(product_ref.shape, f32)

    for here, there in plan.blocks(p):
        shrunk = shrink(plan, p, scale, kept_ref, came_ref, ahead_ref, here)
        ahead = shrunk + momentum * (shrunk - weights_ref[:, here])
        new_weights_ref[:, here] = shrunk
        new_ahead_ref[:, here] = ahead
        total = total + dot_nt(ahead.astype(bf16), act_ref[:, there])
    product_ref[...] = total


def last_kernel(plan, mask_ref, own_ref, other_ref, *refs):
    *refs, out_ref, held_ref, sem = refs
    scale = scale_of(plan, own_ref, other_ref)
    h = plan.height
    copies = []
    for p in (PARTS - 1, *range(1, PARTS - 1), 0):
        kept_ref, came_ref, ahead_ref = refs[3 * p : 3 * p + 3]
        for here, there in plan.blocks(p):
            shrunk = shrink(plan, p, scale, kept_ref, came_ref, ahead_ref, here)
            for g in range(plan.places):
                rows = pl.ds(pl.multiple_of((g ^ mask_ref[0]) * h, h), h)
                held_ref[rows, there] = shrunk[h * g : h * (g + 1)]
        a, b = plan.spans[p]
        copies.append(pltpu.make_async_copy(held_ref.at[:, a:b], out_ref.at[:, a:b], sem.at[p]))
        copies[-1].start()
    for copy in copies:
        copy.wait()


def after(x, earlier):
    return lax.optimization_barrier((x, *earlier))[0]


def all_sum(plan, pieces):
    current = [kept for kept, _ in pieces]
    sends = [sent for _, sent in pieces]
    for stage in range(plan.rows_bits):
        came = [swap(sends[p], "tok", plan.scatter[p][stage]) for p in range(PARTS)]
        for p in range(PARTS):
            arrived = after(came[p], sends[:p]) if p else came[p]
            whole = current[p] + arrived.astype(f32)
            middle = whole.shape[0] // 2 if stage + 1 < plan.rows_bits else 0
            sends[p] = whole[middle:].astype(bf16)
            current[p] = whole[:middle]
    came = [None] * PARTS
    for bit in range(plan.rows_bits, bits_of("tok")):
        if bit > plan.rows_bits:
            sends = [(a.astype(f32) + b.astype(f32)).astype(bf16) for a, b in zip(sends, came)]
        came = [swap(x, "tok", bit) for x in sends]
    square = ()
    for p, width in enumerate(plan.widths):
        last = p + 1 == PARTS
        outs = [((plan.height, width + LANES * last), bf16)] + [((plan.height, LANES), f32)] * (not last)
        current[p], *square = run(
            functools.partial(combine_kernel, plan, p), "combine", outs, [VMEM] * (2 + len(square)), (sends[p], came[p], *square)
        )
    for stage in range(plan.rows_bits):
        came = [swap(current[p], "tok", plan.gather[p][stage]) for p in range(PARTS)]
        if stage + 1 < plan.rows_bits:
            for p in range(PARTS):
                rows, width = current[p].shape
                arrived = after(came[p], current[:p]) if p else came[p]
                if p + 1 < PARTS:
                    current[p] = jnp.concatenate([current[p], arrived], 0)
                else:
                    (current[p],) = run(
                        functools.partial(join_kernel, plan), "join", [((2 * rows, width), bf16)], [VMEM] * 2, (current[p], arrived)
                    )
    return list(zip(current, came))


def across_features(x):
    count = bits_of("feat")
    for bit in range(count - 1):
        x = x + swap(x, "feat", bit)
    return x, swap(x, "feat", count - 1)


def shards(activations, dense_rows, targets):
    rows, columns = dense_rows.shape
    tokens = activations.shape[0]
    plan = Plan(rows, columns, tokens)
    momentum = momentum_terms(ITERS)
    mask = plan.mask().reshape(1).astype(jnp.int32)
    states = [((rows, width), f32) for width in plan.widths]
    small = ((rows, tokens), f32)

    ahead = run(functools.partial(start_kernel, plan), "start", states, [SMEM, VMEM], (mask, dense_rows))
    ahead = list(ahead)
    (product,) = run(
        functools.partial(first_kernel, plan), "first", [small], [VMEM] * (PARTS + 1), (*ahead, activations)
    )
    (wanted,) = run(functools.partial(order_kernel, plan), "order", [small], [SMEM, VMEM], (mask, targets.T))
    weights = list(ahead)
    for iteration in range(ITERS):
        own, other = across_features(product)
        pieces = [
            run(
                functools.partial(gradient_kernel, plan, p),
                "gradient",
                [((rows // 2, plan.widths[p]), f32), ((rows // 2, plan.widths[p]), bf16)],
                [VMEM] * 4,
                (own, other, wanted, activations),
            )
            for p in range(PARTS)
        ]
        halves = all_sum(plan, pieces)
        kept, came = halves[-1]
        last = plan.widths[-1]
        own, other = across_features(kept[:8, last:].astype(f32) + came[:8, last:].astype(f32))
        if iteration + 1 < ITERS:
            before = ()
            for p in (PARTS - 1, *range(1, PARTS - 1), 0):
                weights[p], ahead[p], product = run(
                    functools.partial(update_kernel, plan, p, momentum[iteration]),
                    "update",
                    [states[p], states[p], small],
                    [VMEM] * (7 + len(before)),
                    (own, other, *halves[p], weights[p], ahead[p], activations, *before),
                )
                before = (product,)
        else:
            args = [x for p in range(PARTS) for x in (*halves[p], ahead[p])]
            (result,) = run(
                functools.partial(last_kernel, plan),
                "last",
                [((rows, columns), f32)],
                [SMEM] + [VMEM] * (2 + len(args)),
                (mask, own, other, *args),
                HBM,
                [pltpu.VMEM((rows, columns), f32), pltpu.SemaphoreType.DMA((PARTS,))],
                VMEM_BYTES + 4 * rows * columns,
            )
    return result


def solution(mesh):
    in_specs = (P("tok", "feat"), P(None, "feat"), P("tok", None))
    out_specs = P(None, "feat")
    return jax.shard_map(shards, mesh=mesh, in_specs=in_specs, out_specs=out_specs, check_vma=False)
```

```python
import functools
import math

import jax
import jax.numpy as jnp
from jax import lax
from jax.experimental import pallas as pl
from jax.experimental.pallas import tpu as pltpu
from jax.sharding import PartitionSpec as P

ITERS = 4
STEP = 0.25
THRESHOLD = 0.2
EPSILON = 1e-06
GROUP = 8
SHARES = (16, 16, 16, 8)
PARTS = len(SHARES)
LANES = 128
VMEM_BYTES = 4 * 1024 * 1024

f32 = jnp.float32
bf16 = jnp.bfloat16


def momentum_terms(iterations):
    values = []
    current = 1.0
    for _ in range(iterations):
        upcoming = (1.0 + math.sqrt(1.0 + 4.0 * current * current)) / 2.0
        values.append((current - 1.0) / upcoming)
        current = upcoming
    return values


def swap(x, axis, bit):
    pairs = [(i, i ^ (1 << bit)) for i in range(lax.axis_size(axis))]
    return lax.ppermute(x, axis, pairs)


def bits_of(axis):
    return lax.axis_size(axis).bit_length() - 1


class Plan:
    def __init__(self, rows, columns, tokens):
        self.rows = rows
        self.columns = columns
        self.tokens = tokens
        self.rows_bits = min(bits_of("tok"), (rows // GROUP).bit_length() - 1)
        self.places = 1 << self.rows_bits
        self.height = rows >> self.rows_bits
        self.unit = next(u for u in (256, 128) if columns % u == 0)
        units = columns // self.unit
        self.entries = rows * columns * lax.axis_size("feat")
        self.factor = (columns * lax.axis_size("feat")) ** (-0.5)
        marks = [0]
        for share in SHARES:
            marks.append(marks[-1] + share)
        edges = [self.unit * round(units * m / marks[-1]) for m in marks]
        self.spans = list(zip(edges[:-1], edges[1:]))
        self.widths = [b - a for a, b in self.spans]
        levels = range(self.rows_bits)
        self.scatter = [[(p + s) % self.rows_bits for s in levels] for p in range(PARTS)]
        self.gather = [[(p + s) % self.rows_bits for s in levels] for p in range(PARTS)]

    def blocks(self, p):
        a, b = self.spans[p]
        return [(slice(x - a, x - a + self.unit), slice(x, x + self.unit)) for x in range(a, b, self.unit)]

    def bit_value(self, level):
        return self.places >> (level + 1)

    def arrangement(self, levels):
        result = [0]
        for level in levels:
            result = result + [g + self.bit_value(level) for g in result]
        return result

    def mask(self):
        index = lax.axis_index("tok")
        return sum(((index >> level) & 1) * self.bit_value(level) for level in range(self.rows_bits))

    def rearranged(self, x, places):
        h = self.height
        return jnp.concatenate([x[h * g : h * (g + 1)] for g in places], 0)

    def to_part(self, p, x):
        return self.rearranged(x, self.arrangement(self.scatter[p][::-1]))

    def from_part(self, p, x):
        order = self.arrangement(self.gather[p])
        return self.rearranged(x, [order.index(g) for g in range(self.places)])


def dot_nt(a, b):
    return lax.dot_general(a, b, (((1,), (1,)), ((), ())), preferred_element_type=f32)


VMEM = pl.BlockSpec(memory_space=pltpu.VMEM)
HBM = pl.BlockSpec(memory_space=pltpu.HBM)
SMEM = pl.BlockSpec(memory_space=pltpu.SMEM)


def run(kernel, name, outs, specs, args, place=VMEM, scratch=(), limit=VMEM_BYTES):
    return pl.pallas_call(
        kernel,
        out_shape=tuple(jax.ShapeDtypeStruct(shape, dtype) for shape, dtype in outs),
        in_specs=list(specs),
        out_specs=(place,) * len(outs),
        scratch_shapes=list(scratch),
        compiler_params=pltpu.CompilerParams(vmem_limit_bytes=limit),
        name=name,
    )(*args)


def order_kernel(plan, mask_ref, targets_ref, wanted_ref):
    h = plan.height
    for g in range(plan.places):
        rows = pl.ds(pl.multiple_of((g ^ mask_ref[0]) * h, h), h)
        wanted_ref[g * h : (g + 1) * h] = targets_ref[rows, :]


def start_kernel(plan, mask_ref, dense_ref, *start_refs):
    h = plan.height
    for p in range(PARTS):
        for g in range(plan.places):
            rows = pl.ds(pl.multiple_of((g ^ mask_ref[0]) * h, h), h)
            for here, there in plan.blocks(p):
                start_refs[p][g * h : (g + 1) * h, here] = dense_ref[rows, there]


def first_kernel(plan, *refs):
    *start_refs, act_ref, product_ref = refs
    total = jnp.zeros(product_ref.shape, f32)
    for p in range(PARTS):
        for here, there in plan.blocks(p):
            total = total + dot_nt(start_refs[p][:, here].astype(bf16), act_ref[:, there])
    product_ref[...] = total


def gradient_kernel(plan, p, own_ref, other_ref, wanted_ref, act_ref, keep_ref, send_ref):
    residual = plan.factor * (own_ref[...] + other_ref[...]) - wanted_ref[...]
    half = plan.rows // 2
    arranged = plan.to_part(p, residual).astype(bf16)

    for here, there in plan.blocks(p):
        block = jnp.dot(arranged, act_ref[:, there], preferred_element_type=f32)
        keep_ref[:, here] = block[:half]
        send_ref[:, here] = block[half:].astype(bf16)


def pair_tile(value, rows):
    value = jnp.broadcast_to(value, (rows, LANES))
    high = value.astype(bf16).astype(f32)
    lane = lax.broadcasted_iota(jnp.int32, (rows, LANES), 1)
    return jnp.where(lane < LANES // 2, high, value - high).astype(bf16)


def pair_value(tile):
    tile = tile.astype(f32)
    return jnp.sum(tile, keepdims=True) / (tile.shape[0] * (LANES // 2))


def combine_kernel(plan, p, low_ref, came_ref, *refs):
    total = refs[0][...] if p else jnp.zeros((plan.height, LANES), f32)
    out_ref = refs[1] if p else refs[0]
    for here, _ in plan.blocks(p):
        block = (low_ref[:, here].astype(f32) + came_ref[:, here].astype(f32)).astype(bf16)
        out_ref[:, here] = block
        block = block.astype(f32)
        for lane in range(0, plan.unit, LANES):
            piece = block[:, lane : lane + LANES]
            total = total + piece * piece
    if p + 1 < PARTS:
        refs[-1][...] = total
    else:
        out_ref[:, plan.widths[p] :] = pair_tile(jnp.sum(total, keepdims=True), plan.height)


def join_kernel(plan, own_ref, came_ref, out_ref):
    h, width = own_ref.shape
    last = width - LANES
    for start in range(0, last, plan.unit):
        here = slice(start, start + plan.unit)
        out_ref[:, here] = jnp.concatenate([own_ref[:, here].astype(f32), came_ref[:, here].astype(f32)], 0).astype(bf16)
    square = pair_value(own_ref[:, last:]) + pair_value(came_ref[:, last:])
    out_ref[:, last:] = pair_tile(square, 2 * h)


def scale_of(plan, own_ref, other_ref):
    mean_square = pair_value(own_ref[...] + other_ref[...]) / plan.entries
    return STEP * lax.rsqrt(mean_square + EPSILON)


def shrink(plan, p, scale, kept_ref, came_ref, ahead_ref, here):
    gradient = jnp.concatenate([kept_ref[:, here].astype(f32), came_ref[:, here].astype(f32)], 0)
    moved = ahead_ref[:, here] - scale * plan.from_part(p, gradient)
    return moved - jnp.clip(moved, -THRESHOLD, THRESHOLD)


def update_kernel(plan, p, momentum, *refs):
    own_ref, other_ref, kept_ref, came_ref, weights_ref, ahead_ref, act_ref, *refs = refs
    *before, new_weights_ref, new_ahead_ref, product_ref = refs
    scale = scale_of(plan, own_ref, other_ref)
    total = before[0][...] if before else jnp.zeros(product_ref.shape, f32)

    for here, there in plan.blocks(p):
        shrunk = shrink(plan, p, scale, kept_ref, came_ref, ahead_ref, here)
        ahead = shrunk + momentum * (shrunk - weights_ref[:, here])
        new_weights_ref[:, here] = shrunk
        new_ahead_ref[:, here] = ahead
        total = total + dot_nt(ahead.astype(bf16), act_ref[:, there])
    product_ref[...] = total


def last_kernel(plan, mask_ref, own_ref, other_ref, *refs):
    *refs, out_ref, held_ref, sem = refs
    scale = scale_of(plan, own_ref, other_ref)
    h = plan.height
    copies = []
    for p in (PARTS - 1, *range(1, PARTS - 1), 0):
        kept_ref, came_ref, ahead_ref = refs[3 * p : 3 * p + 3]
        for here, there in plan.blocks(p):
            shrunk = shrink(plan, p, scale, kept_ref, came_ref, ahead_ref, here)
            for g in range(plan.places):
                rows = pl.ds(pl.multiple_of((g ^ mask_ref[0]) * h, h), h)
                held_ref[rows, there] = shrunk[h * g : h * (g + 1)]
        a, b = plan.spans[p]
        copies.append(pltpu.make_async_copy(held_ref.at[:, a:b], out_ref.at[:, a:b], sem.at[p]))
        copies[-1].start()
    for copy in copies:
        copy.wait()


def after(x, earlier):
    return lax.optimization_barrier((x, *earlier))[0]


def all_sum(plan, pieces):
    current = [kept for kept, _ in pieces]
    sends = [sent for _, sent in pieces]
    for stage in range(plan.rows_bits):
        came = [swap(sends[p], "tok", plan.scatter[p][stage]) for p in range(PARTS)]
        for p in range(PARTS):
            arrived = after(came[p], sends[:p]) if p else came[p]
            whole = current[p] + arrived.astype(f32)
            middle = whole.shape[0] // 2 if stage + 1 < plan.rows_bits else 0
            sends[p] = whole[middle:].astype(bf16)
            current[p] = whole[:middle]
    came = [None] * PARTS
    for bit in range(plan.rows_bits, bits_of("tok")):
        if bit > plan.rows_bits:
            sends = [(a.astype(f32) + b.astype(f32)).astype(bf16) for a, b in zip(sends, came)]
        came = [swap(after(x, sends[:p]) if p else x, "tok", bit) for p, x in enumerate(sends)]
    square = ()
    for p, width in enumerate(plan.widths):
        last = p + 1 == PARTS
        outs = [((plan.height, width + LANES * last), bf16)] + [((plan.height, LANES), f32)] * (not last)
        current[p], *square = run(
            functools.partial(combine_kernel, plan, p), "combine", outs, [VMEM] * (2 + len(square)), (sends[p], came[p], *square)
        )
    for stage in range(plan.rows_bits):
        came = [swap(current[p], "tok", plan.gather[p][stage]) for p in range(PARTS)]
        if stage + 1 < plan.rows_bits:
            for p in range(PARTS):
                rows, width = current[p].shape
                arrived = after(came[p], current[:p]) if p else came[p]
                if p + 1 < PARTS:
                    current[p] = jnp.concatenate([current[p], arrived], 0)
                else:
                    (current[p],) = run(
                        functools.partial(join_kernel, plan), "join", [((2 * rows, width), bf16)], [VMEM] * 2, (current[p], arrived)
                    )
    return list(zip(current, came))


def across_features(x):
    count = bits_of("feat")
    for bit in range(count - 1):
        x = x + swap(x, "feat", bit)
    return x, swap(x, "feat", count - 1)


def shards(activations, dense_rows, targets):
    rows, columns = dense_rows.shape
    tokens = activations.shape[0]
    plan = Plan(rows, columns, tokens)
    momentum = momentum_terms(ITERS)
    mask = plan.mask().reshape(1).astype(jnp.int32)
    states = [((rows, width), f32) for width in plan.widths]
    small = ((rows, tokens), f32)

    ahead = run(functools.partial(start_kernel, plan), "start", states, [SMEM, VMEM], (mask, dense_rows))
    ahead = list(ahead)
    (product,) = run(
        functools.partial(first_kernel, plan), "first", [small], [VMEM] * (PARTS + 1), (*ahead, activations)
    )
    (wanted,) = run(functools.partial(order_kernel, plan), "order", [small], [SMEM, VMEM], (mask, targets.T))
    weights = list(ahead)
    for iteration in range(ITERS):
        own, other = across_features(product)
        pieces = [
            run(
                functools.partial(gradient_kernel, plan, p),
                "gradient",
                [((rows // 2, plan.widths[p]), f32), ((rows // 2, plan.widths[p]), bf16)],
                [VMEM] * 4,
                (own, other, wanted, activations),
            )
            for p in range(PARTS)
        ]
        halves = all_sum(plan, pieces)
        kept, came = halves[-1]
        last = plan.widths[-1]
        own, other = across_features(kept[:8, last:].astype(f32) + came[:8, last:].astype(f32))
        if iteration + 1 < ITERS:
            before = ()
            for p in (PARTS - 1, *range(1, PARTS - 1), 0):
                weights[p], ahead[p], product = run(
                    functools.partial(update_kernel, plan, p, momentum[iteration]),
                    "update",
                    [states[p], states[p], small],
                    [VMEM] * (7 + len(before)),
                    (own, other, *halves[p], weights[p], ahead[p], activations, *before),
                )
                before = (product,)
        else:
            args = [x for p in range(PARTS) for x in (*halves[p], ahead[p])]
            (result,) = run(
                functools.partial(last_kernel, plan),
                "last",
                [((rows, columns), f32)],
                [SMEM] + [VMEM] * (2 + len(args)),
                (mask, own, other, *args),
                HBM,
                [pltpu.VMEM((rows, columns), f32), pltpu.SemaphoreType.DMA((PARTS,))],
                VMEM_BYTES + 4 * rows * columns,
            )
    return result


def solution(mesh):
    in_specs = (P("tok", "feat"), P(None, "feat"), P("tok", None))
    out_specs = P(None, "feat")
    return jax.shard_map(shards, mesh=mesh, in_specs=in_specs, out_specs=out_specs, check_vma=False)
```
